32 devices in a mesh: dp: 8 (over z, y), fsdp: 2 (over x), section: 2 (over core).
Axes of the slice: x: 2, y: 2, z: 4, core: 2. Of those that a mesh axis runs over, the one named last changes fastest.
Arguments:
- acts: bfloat16 [8192, 5120], P(('dp', 'section'), 'fsdp'), may hold values from -100 to 100
- output_gradient: bfloat16 [8192, 1024], P(('dp', 'section'), 'fsdp'), may hold values from -40 to 40
- lengths: int32 [32], P(('dp', 'section')), may hold values from 1 to 256
- buckets: int32 [32], P(('dp', 'section')), may hold values from 0 to 3
- frozen_key_weight: bfloat16 [5120, 1024], P('fsdp'), may hold values from -0.078125 to 0.078125
- adapter_down_weight: float32 [5120, 128], P('fsdp'), may hold values from -0.078125 to 0.078125
- adapter_up_weight: float32 [128, 1024], P(None, 'fsdp'), may hold values from -0.5 to 0.5
- prompts: bfloat16 [8192, 5120], P(('dp', 'section'), 'fsdp'), may hold values from -6 to 6
Outputs:
- input_gradient: bfloat16 [8192, 5120], P(('dp', 'section'), 'fsdp')
- next_down_weight: float32 [5120, 128], P('fsdp')
- next_up_weight: float32 [128, 1024], P(None, 'fsdp')
- keys: bfloat16 [8192, 1024], P(('dp', 'section'), 'fsdp')
The draws below stay inside these ranges and needn't reach their ends.
All inputs are finite; a program needn't handle non-finite values.
Results may differ from the reference program's by a relative error of at most 0.0059.
Values may be sent and summed in bfloat16 or wider, within the bound.
A program may use at most 128 MiB of HBM per device.

```python
import jax
import jax.numpy as jnp
from jax import lax

MODEL_WIDTH = 5120
KEY_CHANNELS = 1024
ADAPTER_RANK = 128
SLOT = 256
SEQS = 32
TOKENS = 8192
PROMPTS = 8192


def rising_scale(key, count, reach, jitter):
    ramp = jnp.arange(count, dtype=jnp.int32).astype(jnp.float32) / jnp.float32(max(count - 1, 1))
    noise = jax.random.uniform(key, (1, count), jnp.float32, -jitter, jitter)
    return jnp.exp(reach * (2.0 * ramp[None, :] - 1.0) + noise)


def draw_acts(key, part):
    key = jax.random.fold_in(key, 11)
    key_rows, key_cols, key_base = jax.random.split(key, 3)
    row_scale = jnp.exp(jax.random.uniform(key_rows, (TOKENS, 1), jnp.float32, -0.8, 0.8))
    col_scale = rising_scale(key_cols, MODEL_WIDTH, 1.0, 0.5)
    base_vals = jnp.clip(jax.random.normal(key_base, (TOKENS, MODEL_WIDTH), jnp.float32), -6.0, 6.0)
    return (base_vals * row_scale * col_scale).astype(jnp.bfloat16)


def draw_output_gradient(key, part):
    key = jax.random.fold_in(key, 23)
    key_cols, key_base = jax.random.split(key, 2)
    col_scale = rising_scale(key_cols, KEY_CHANNELS, 0.9, 0.4)
    base_vals = jnp.clip(jax.random.normal(key_base, (TOKENS, KEY_CHANNELS), jnp.float32), -6.0, 6.0)
    return (base_vals * col_scale).astype(jnp.bfloat16)


def with_ends(values, rng, least, largest):
    dims = values.shape
    index_at = [jax.random.randint(jax.random.fold_in(rng, axis), (), 0, dims[axis]) for axis in range(len(dims))]
    values = values.at[tuple(index_at)].set(least)
    longest = dims.index(max(dims))
    index_at[longest] = (index_at[longest] + 1) % dims[longest]
    return values.at[tuple(index_at)].set(largest)


def shard_levels(key, shape, pieces, smallest, top_value):
    def one(position, parts):
        draws = jax.random.uniform(jax.random.fold_in(jax.random.fold_in(key, 6), position), (parts,), jnp.float32, smallest / len(pieces), top_value / len(pieces))
        return jnp.repeat(jnp.exp(draws), shape[position] // parts).reshape((-1,) + (1,) * (len(shape) - position - 1))

    gain = one(*pieces[0])
    for cut in pieces[1:]:
        gain = gain * one(*cut)
    return gain


def bell_draw(stream_key, shape, deviation, most, cuts=(), kind=jnp.bfloat16):
    drawn = deviation * jax.random.normal(stream_key, shape, jnp.float32)
    if cuts:
        drawn = drawn * shard_levels(stream_key, shape, cuts, -0.22, 0.18)
    return jnp.clip(drawn, -most, most).astype(kind)


def setup_inputs(seed: int = 0) -> dict:
    splits = jax.random.split(jax.random.key(seed), 9)
    acts = draw_acts(jax.random.fold_in(splits[8], 71), 0)
    output_gradient = draw_output_gradient(jax.random.fold_in(splits[8], 71), 0)
    lengths = with_ends(jax.random.randint(splits[2], (SEQS,), 1, SLOT + 1), jax.random.fold_in(splits[2], 1), 1, SLOT).astype(jnp.int32)
    buckets = with_ends(jax.random.randint(splits[3], (SEQS,), 0, 4), jax.random.fold_in(splits[3], 1), 0, 3).astype(jnp.int32)
    frozen_key_weight = bell_draw(splits[4], (MODEL_WIDTH, KEY_CHANNELS), MODEL_WIDTH ** -0.5, 0.078125, ((0, 2),))
    adapter_down_weight = bell_draw(splits[5], (MODEL_WIDTH, ADAPTER_RANK), MODEL_WIDTH ** -0.5, 0.078125, ((0, 2),), jnp.float32)
    adapter_up_weight = bell_draw(splits[6], (ADAPTER_RANK, KEY_CHANNELS), ADAPTER_RANK ** -0.5, 0.5, ((1, 2),), jnp.float32)
    prompts = bell_draw(splits[7], (PROMPTS, MODEL_WIDTH), 1.0, 6.0, ((0, 16), (1, 2)))
    return {"acts": acts, "output_gradient": output_gradient, "lengths": lengths, "buckets": buckets, "frozen_key_weight": frozen_key_weight, "adapter_down_weight": adapter_down_weight, "adapter_up_weight": adapter_up_weight, "prompts": prompts}


adapter_scale = 0.5
step_rate = 16.0
clip_norm = 1.0

def reference(acts, output_gradient, lengths, buckets, frozen_key_weight, adapter_down_weight, adapter_up_weight, prompts):
    slot_pos = jnp.arange(TOKENS, dtype=jnp.int32) % SLOT
    seq_len = jnp.repeat(lengths, SLOT)
    advantage = jnp.repeat(buckets.astype(jnp.float32) - 1.5, SLOT)
    token_weight = jnp.where(slot_pos < seq_len, advantage, jnp.float32(0.0))
    key_gradient = (token_weight[:, None] * output_gradient.astype(jnp.float32)).astype(jnp.bfloat16)
    first_factor_half = adapter_down_weight.astype(jnp.bfloat16)
    second_factor_half = adapter_up_weight.astype(jnp.bfloat16)
    down_acts = jnp.dot(acts, first_factor_half, preferred_element_type=jnp.float32)
    up_grads = jnp.dot(key_gradient, second_factor_half.T, preferred_element_type=jnp.float32)
    down_weight_half = down_acts.astype(jnp.bfloat16)
    up_weight_half = up_grads.astype(jnp.bfloat16)
    up_gradient = adapter_scale * jnp.dot(down_weight_half.T, key_gradient, preferred_element_type=jnp.float32)
    down_gradient = adapter_scale * jnp.dot(acts.T, up_weight_half, preferred_element_type=jnp.float32)
    squares = jnp.sum(down_gradient * down_gradient) + jnp.sum(up_gradient * up_gradient)
    norm = jnp.sqrt(squares + 1e-12)
    scale_factor = step_rate * jnp.minimum(1.0, clip_norm / norm)
    next_down_weight = adapter_down_weight - scale_factor * down_gradient
    next_up_weight = adapter_up_weight - scale_factor * up_gradient
    input_gradient = jnp.dot(key_gradient, frozen_key_weight.T, preferred_element_type=jnp.float32)
    input_gradient = input_gradient + adapter_scale * jnp.dot(up_weight_half, first_factor_half.T, preferred_element_type=jnp.float32)
    weight_change = jnp.dot(next_down_weight, next_up_weight, precision=lax.Precision.HIGHEST)
    combined_weight = (frozen_key_weight.astype(jnp.float32) + adapter_scale * weight_change).astype(jnp.bfloat16)
    keys = jnp.dot(prompts, combined_weight, preferred_element_type=jnp.float32).astype(jnp.bfloat16)
    return (input_gradient.astype(jnp.bfloat16), next_down_weight, next_up_weight, keys)
```

```python
import functools

import jax
import jax.numpy as jnp
from jax import lax
from jax.experimental import pallas as pl
from jax.experimental.pallas import tpu as pltpu
from jax.sharding import PartitionSpec as P

ADAPTER_SCALE = 0.5
STEP_RATE = 16.0
CLIP_NORM = 1.0
MESH = pl.DeviceIdType.MESH
F32 = jnp.float32
BF16 = jnp.bfloat16
NT = (((1,), (1,)), ((), ()))


class Plan:
    def __init__(self, mesh, rows, width, channels, rank):
        self.fsdp = mesh.shape["fsdp"]
        self.cores = mesh.shape["section"]
        dp = mesh.shape["dp"]
        self.outer = 4 if dp % 4 == 0 else 1
        self.inner = dp // self.outer
        self.rows, self.width, self.channels, self.rank = rows, width, channels, rank
        span = self.cores * self.inner
        self.unit = 256 if width % 256 == 0 and channels % 256 == 0 else 128
        units = (width + channels) // self.unit
        self.chunks = -(-units // span)
        self.down_units = width // self.unit
        self.units = units
        self.tile = 256 if width % 256 == 0 else 128


def kernel(
    plan,
    lengths, buckets, acts_h, og_h, frozen_h, down_h, up_h, prompts_h,
    ig_h, nd_h, nu_h, keys_h,
    acts, og, frozen, down, up, prompts,
    a_half, gk, proj_send, proj_recv, pd, pg,
    kp_own, kp_send, kp_recv,
    gbuf, core_recv, y_send, y_recv, quarter, z_send, z_recv, ag, sq,
    ig, nd, nu, keys,
    load_sem, store_sem, x_send_sem, x_recv_sem, d_send_sem, d_recv_sem, q_send_sem, q_recv_sem,
):
    F, S, I, O, K = plan.fsdp, plan.cores, plan.inner, plan.outer, plan.chunks
    U, W, C = plan.unit, plan.width, plan.channels
    T = plan.rows
    x = lax.axis_index("fsdp")
    dp = lax.axis_index("dp")
    core = lax.axis_index("section")
    zi, yi = dp // I, dp % I

    loads = {}
    for n, (name, src, dst) in enumerate((
        ("og", og_h, og), ("up", up_h, up), ("acts", acts_h, acts), ("down", down_h, down),
        ("prompts", prompts_h, prompts), ("frozen", frozen_h, frozen),
    )):
        loads[name] = pltpu.make_async_copy(src, dst, load_sem.at[n])
        loads[name].start()

    x_peer = [lax.rem(x + d, F) for d in range(F)]
    x_from = [lax.rem(x + F - d, F) for d in range(F)]
    y_peer = [lax.rem(yi + d, I) for d in range(I)]
    y_from = [lax.rem(yi + I - d, I) for d in range(I)]
    z_peer = [lax.rem(zi + d, O) for d in range(O)]
    z_from = [lax.rem(zi + O - d, O) for d in range(O)]

    def x_id(d):
        return {"fsdp": x_peer[d]}

    def y_id(d):
        return {"dp": zi * I + y_peer[d]}

    def z_id(d):
        return {"dp": z_peer[d] * I + yi}

    core_id = {"section": 1 - core}
    others = (
        [x_id(d) for d in range(1, F)] + [y_id(d) for d in range(1, I)]
        + [z_id(d) for d in range(1, O)] + [core_id]
    )
    barrier = pltpu.get_barrier_semaphore()
    for other in others:
        pl.semaphore_signal(barrier, inc=1, device_id=other, device_id_type=MESH)

    sent = []

    def send(src, dst, ssem, rsem, to):
        copy = pltpu.make_async_remote_copy(
            src_ref=src, dst_ref=dst, send_sem=ssem, recv_sem=rsem, device_id=to, device_id_type=MESH
        )
        copy.start()
        sent.append(copy)

    def arrive(src, dst, ssem, rsem, to):
        pltpu.make_async_remote_copy(
            src_ref=src, dst_ref=dst, send_sem=ssem, recv_sem=rsem, device_id=to, device_id_type=MESH
        ).wait_recv()

    def proj_exchange(n, value):
        proj_send[n] = value.astype(BF16)
        for d in range(1, F):
            send(proj_send.at[n], proj_recv.at[n, d], x_send_sem.at[n, d], x_recv_sem.at[n, d], x_id(d))

    def proj_sum(n, value):
        for d in range(1, F):
            arrive(proj_send.at[n], proj_recv.at[n, d], x_send_sem.at[n, d], x_recv_sem.at[n, d], x_id(d))
            value = value + proj_recv[n, d].astype(F32)
        return value

    loads["og"].wait()
    loads["up"].wait()
    slot = T // lengths.shape[0]
    position = lax.broadcasted_iota(jnp.int32, (slot, C), 0)
    for i in range(lengths.shape[0]):
        weight = jnp.where(position < lengths[i], buckets[i].astype(F32) - 1.5, 0.0)
        block = og[i * slot:(i + 1) * slot, :].astype(F32)
        gk[x, i * slot:(i + 1) * slot, :] = (weight * block).astype(BF16)
    mine = gk[x]
    up_part = lax.dot_general(mine, up[...].astype(BF16), NT, preferred_element_type=F32)
    pl.semaphore_wait(barrier, len(others))
    proj_exchange(0, up_part)

    loads["acts"].wait()
    loads["down"].wait()
    a_half[...] = down[...].astype(BF16)
    down_part = jnp.dot(acts[...], a_half[...], preferred_element_type=F32)
    proj_exchange(1, down_part)

    loads["prompts"].wait()
    loads["frozen"].wait()
    tile_c = min(256, C)

    def frozen_part(owner, put):
        @pl.loop(0, C // tile_c)
        def _(t):
            cols = pl.ds(pl.multiple_of(t * tile_c, tile_c), tile_c)
            src = pl.ds(pl.multiple_of(owner * C + t * tile_c, tile_c), tile_c)
            put(cols, jnp.dot(prompts[...], frozen[:, src], preferred_element_type=F32))

    for d in range(1, F):
        def put_other(cols, value, d=d):
            kp_send[d, :, cols] = value.astype(BF16)

        frozen_part(x_peer[d], put_other)

    up_half = proj_sum(0, up_part)
    up_half_t = up_half.T.astype(BF16)
    up_half = up_half.astype(BF16)
    down_half_t = None

    def core_copy(k):
        return (gbuf.at[k, 1 - core], core_recv.at[k], d_send_sem.at[k, 0], d_recv_sem.at[k, 0], core_id)

    for k in range(K):
        for s in range(S):
            for i in range(I):
                n = (k * S + s) * I + i
                if n < plan.down_units:
                    part = jnp.dot(up_half_t, acts[:, n * U:(n + 1) * U], preferred_element_type=F32)
                elif n < plan.units:
                    if down_half_t is None:
                        down_half_t = proj_sum(1, down_part).T.astype(BF16)
                    m = n - plan.down_units
                    part = jnp.dot(down_half_t, gk[x, :, m * U:(m + 1) * U], preferred_element_type=F32)
                else:
                    part = jnp.zeros((plan.rank, U), F32)
                gbuf[k, s, i] = ADAPTER_SCALE * part
        send(*core_copy(k))

    for d in range(1, F):
        send(gk.at[x], gk.at[x], x_send_sem.at[2, d], x_recv_sem.at[2, d], x_id(d))
    for d in range(1, F):
        send(kp_send.at[d], kp_recv.at[d], x_send_sem.at[3, d], x_recv_sem.at[3, d], x_id(d))

    def y_copy(k, d):
        return (y_send.at[k, d], y_recv.at[k, d], d_send_sem.at[k, d], d_recv_sem.at[k, d], y_id(d))

    def z_copy(k, d):
        e = I + d
        return (z_send.at[k, z_peer[d]], z_recv.at[k, d], d_send_sem.at[k, e], d_recv_sem.at[k, e], z_id(d))

    for k in range(K):
        arrive(*core_copy(k))
        for d in range(I):
            value = gbuf[k, core, y_peer[d]] + core_recv[k, y_peer[d]]
            if d == 0:
                quarter[k] = value
            else:
                y_send[k, d] = value.astype(BF16)
                send(*y_copy(k, d))

    def put_own(cols, value):
        kp_own[:, cols] = value

    frozen_part(x, put_own)
    pd[...] = jnp.dot(prompts[...], a_half[...], preferred_element_type=F32)

    part_rows = plan.rank // O
    for k in range(K):
        value = quarter[k]
        for d in range(1, I):
            arrive(*y_copy(k, d))
            value = value + y_recv[k, d].astype(F32)
        quarter[k] = value
        for o in range(O):
            z_send[k, o] = value[o * part_rows:(o + 1) * part_rows].astype(BF16)
        for d in range(1, O):
            send(*z_copy(k, d))

    base = I + O

    def ag_z(k, d, slot):
        e = base + d
        return (ag.at[k, core, yi, zi], ag.at[k, core, yi, slot], d_send_sem.at[k, e], d_recv_sem.at[k, e], z_id(d))

    def ag_y(k, d, slot):
        e = base + O + d
        return (ag.at[k, core, yi], ag.at[k, core, slot], d_send_sem.at[k, e], d_recv_sem.at[k, e], y_id(d))

    def ag_core(k, slot):
        e = base + O + I
        return (ag.at[k, core], ag.at[k, slot], d_send_sem.at[k, e], d_recv_sem.at[k, e], core_id)

    squares = jnp.zeros((part_rows, U), F32)
    for k in range(K):
        value = quarter[k, pl.ds(pl.multiple_of(zi * part_rows, part_rows), part_rows), :]
        for d in range(1, O):
            arrive(*z_copy(k, d))
            value = value + z_recv[k, d].astype(F32)
        rounded = value.astype(BF16)
        ag[k, core, yi, zi] = rounded
        for d in range(1, O):
            send(*ag_z(k, d, zi))
        value = rounded.astype(F32)
        squares = squares + value * value

    def sq_send(stage, value, own, count, to):
        sq[stage, own] = value
        for d in range(1, count):
            send(sq.at[stage, own], sq.at[stage, own], q_send_sem.at[stage, d], q_recv_sem.at[stage, d], to(d))

    def sq_sum(stage, own, count, to, source):
        for d in range(1, count):
            arrive(sq.at[stage, own], sq.at[stage, source(d)], q_send_sem.at[stage, d], q_recv_sem.at[stage, d], to(d))
        total = sq[stage, 0]
        for n in range(1, count):
            total = total + sq[stage, n]
        return total

    total = jnp.broadcast_to(jnp.sum(squares, keepdims=True), (8, 128))
    sq_send(0, total, zi, O, z_id)

    for k in range(K):
        for d in range(1, O):
            arrive(*ag_z(k, d, z_from[d]))
        for d in range(1, I):
            send(*ag_y(k, d, yi))
    total = sq_sum(0, zi, O, z_id, lambda d: z_from[d])
    sq_send(1, total, yi, I, y_id)

    for d in range(1, F):
        arrive(gk.at[x], gk.at[x_from[d]], x_send_sem.at[2, d], x_recv_sem.at[2, d], x_id(d))
    tile = plan.tile

    def ig_tile(t):
        span = pl.ds(pl.multiple_of(t * tile, tile), tile)
        value = ADAPTER_SCALE * lax.dot_general(up_half, a_half[span, :], NT, preferred_element_type=F32)
        for p in range(F):
            value = value + lax.dot_general(
                gk[p], frozen[span, p * C:(p + 1) * C], NT, preferred_element_type=F32
            )
        ig[:, span] = value.astype(BF16)

    pl.loop(0, W // tile)(ig_tile)
    ig_store = pltpu.make_async_copy(ig, ig_h, store_sem.at[0])
    ig_store.start()

    for k in range(K):
        for d in range(1, I):
            arrive(*ag_y(k, d, y_from[d]))
        send(*ag_core(k, core))
    total = sq_sum(1, yi, I, y_id, lambda d: y_from[d])
    sq_send(2, total, core, S, lambda d: core_id)
    total = sq_sum(2, core, S, lambda d: core_id, lambda d: 1 - core)
    sq_send(3, total, x, F, x_id)

    def unit_of(n):
        k, s, i = n // (S * I), (n // I) % S, n % I
        return ag[k, s, i].reshape(plan.rank, U)

    low = jnp.zeros((T, plan.rank), F32)
    for k in range(K):
        arrive(*ag_core(k, 1 - core))
        for n in range(k * S * I, (k + 1) * S * I):
            if n < plan.down_units:
                low = low + lax.dot_general(
                    prompts[:, n * U:(n + 1) * U], unit_of(n), NT, preferred_element_type=F32
                )
    total = sq_sum(3, x, F, x_id, lambda d: x_from[d])
    norm = jnp.sqrt(total + 1e-12)
    factor = (STEP_RATE * jnp.minimum(1.0, CLIP_NORM / norm))[0:1, 0:1]

    pg[...] = pd[...] - factor * low
    proj_exchange(2, pg[...])

    for n in range(plan.units):
        if n < plan.down_units:
            span = slice(n * U, (n + 1) * U)
            nd[span, :] = down[span, :] - factor * unit_of(n).astype(F32).T
        else:
            span = slice((n - plan.down_units) * U, (n - plan.down_units + 1) * U)
            nu[:, span] = up[:, span] - factor * unit_of(n).astype(F32)
    nd_store = pltpu.make_async_copy(nd, nd_h, store_sem.at[1])
    nd_store.start()
    nu_store = pltpu.make_async_copy(nu, nu_h, store_sem.at[2])
    nu_store.start()

    for d in range(1, F):
        arrive(kp_send.at[d], kp_recv.at[d], x_send_sem.at[3, d], x_recv_sem.at[3, d], x_id(d))
        kp_own[...] = kp_own[...] + kp_recv[d].astype(F32)
    low_half = (ADAPTER_SCALE * proj_sum(2, pg[...])).astype(BF16)
    keys[...] = (
        kp_own[...] + jnp.dot(low_half, nu[...].astype(BF16), preferred_element_type=F32)
    ).astype(BF16)
    keys_store = pltpu.make_async_copy(keys, keys_h, store_sem.at[3])
    keys_store.start()

    for copy in sent:
        copy.wait_send()
    ig_store.wait()
    nd_store.wait()
    nu_store.wait()
    keys_store.wait()


def per_device(mesh, acts, output_gradient, lengths, buckets, frozen, down, up, prompts):
    T, W = acts.shape
    C = output_gradient.shape[1]
    R = down.shape[1]
    plan = Plan(mesh, T, W, C, R)
    F, S, I, O, K, U = plan.fsdp, plan.cores, plan.inner, plan.outer, plan.chunks, plan.unit
    N = C * F
    smem = pl.BlockSpec(memory_space=pltpu.SMEM)
    hbm = pl.BlockSpec(memory_space=pl.ANY)
    dma = pltpu.SemaphoreType.DMA
    hops = I + O + O + I + 1
    scratch = [
        pltpu.VMEM((T, W), BF16), pltpu.VMEM((T, C), BF16), pltpu.VMEM((W, N), BF16),
        pltpu.VMEM((W, R), F32), pltpu.VMEM((R, C), F32), pltpu.VMEM((T, W), BF16),
        pltpu.VMEM((W, R), BF16), pltpu.VMEM((F, T, C), BF16),
        pltpu.VMEM((3, T, R), BF16), pltpu.VMEM((3, F, T, R), BF16),
        pltpu.VMEM((T, R), F32), pltpu.VMEM((T, R), F32),
        pltpu.VMEM((T, C), F32), pltpu.VMEM((F, T, C), BF16), pltpu.VMEM((F, T, C), BF16),
        pltpu.VMEM((K, S, I, R, U), F32), pltpu.VMEM((K, I, R, U), F32),
        pltpu.VMEM((K, I, R, U), BF16), pltpu.VMEM((K, I, R, U), BF16),
        pltpu.VMEM((K, R, U), F32),
        pltpu.VMEM((K, O, R // O, U), BF16), pltpu.VMEM((K, O, R // O, U), BF16),
        pltpu.VMEM((K, S, I, O, R // O, U), BF16),
        pltpu.VMEM((4, max(O, I, S, F), 8, 128), F32),
        pltpu.VMEM((T, W), BF16), pltpu.VMEM((W, R), F32), pltpu.VMEM((R, C), F32), pltpu.VMEM((T, C), BF16),
        dma((6,)), dma((4,)), dma((4, F)), dma((4, F)), dma((K, hops)), dma((K, hops)),
        dma((4, max(O, I, S, F))), dma((4, max(O, I, S, F))),
    ]
    return pl.pallas_call(
        functools.partial(kernel, plan),
        out_shape=(
            jax.ShapeDtypeStruct((T, W), BF16),
            jax.ShapeDtypeStruct((W, R), F32),
            jax.ShapeDtypeStruct((R, C), F32),
            jax.ShapeDtypeStruct((T, C), BF16),
        ),
        in_specs=[smem, smem] + [hbm] * 6,
        out_specs=(hbm,) * 4,
        scratch_shapes=scratch,
        compiler_params=pltpu.CompilerParams(
            collective_id=0, has_side_effects=True, vmem_limit_bytes=48 * 1024 * 1024
        ),
        cost_estimate=pl.CostEstimate(
            flops=2 * T * W * (2 * N + 4 * R), bytes_accessed=2 * (3 * T * W + W * N), transcendentals=0
        ),
        name="adapter_step",
    )(lengths, buckets, acts, output_gradient, frozen, down, up, prompts)


def solution(mesh):
    tokens = P(("dp", "section"), "fsdp")
    return jax.shard_map(
        functools.partial(per_device, mesh),
        mesh=mesh,
        in_specs=(
            tokens, tokens, P(("dp", "section")), P(("dp", "section")),
            P("fsdp", None), P("fsdp", None), P(None, "fsdp"), tokens,
        ),
        out_specs=(tokens, P("fsdp", None), P(None, "fsdp"), tokens),
        check_vma=False,
    )
```

```python
import functools

import jax
import jax.numpy as jnp
from jax import lax
from jax.experimental import pallas as pl
from jax.experimental.pallas import tpu as pltpu
from jax.sharding import PartitionSpec as P

ADAPTER_SCALE = 0.5
STEP_RATE = 16.0
CLIP_NORM = 1.0
MESH = pl.DeviceIdType.MESH
F32 = jnp.float32
BF16 = jnp.bfloat16
NT = (((1,), (1,)), ((), ()))


class Plan:
    def __init__(self, mesh, rows, width, channels, rank):
        self.fsdp = mesh.shape["fsdp"]
        self.cores = mesh.shape["section"]
        dp = mesh.shape["dp"]
        self.outer = 4 if dp % 4 == 0 else 1
        self.inner = dp // self.outer
        self.rows, self.width, self.channels, self.rank = rows, width, channels, rank
        span = self.cores * self.inner
        self.unit = 256 if width % 256 == 0 and channels % 256 == 0 else 128
        units = (width + channels) // self.unit
        self.chunks = -(-units // span)
        self.down_units = width // self.unit
        self.units = units
        self.tile = 256 if width % 256 == 0 else 128


def kernel(
    plan,
    lengths, buckets, acts_h, og_h, frozen_h, down_h, up_h, prompts_h,
    ig_h, nd_h, nu_h, keys_h,
    acts, og, frozen, down, up, prompts,
    a_half, gk, proj_send, proj_recv, pd, pg,
    kp_own, kp_send, kp_recv,
    gbuf, core_recv, y_send, y_recv, quarter, z_send, z_recv, ag, sq,
    ig, nd, nu, keys,
    load_sem, store_sem, x_send_sem, x_recv_sem, d_send_sem, d_recv_sem, q_send_sem, q_recv_sem,
):
    F, S, I, O, K = plan.fsdp, plan.cores, plan.inner, plan.outer, plan.chunks
    U, W, C = plan.unit, plan.width, plan.channels
    T = plan.rows
    x = lax.axis_index("fsdp")
    dp = lax.axis_index("dp")
    core = lax.axis_index("section")
    zi, yi = dp // I, dp % I

    loads = {}
    for n, (name, src, dst) in enumerate((
        ("og", og_h, og), ("up", up_h, up), ("acts", acts_h, acts), ("down", down_h, down),
        ("prompts", prompts_h, prompts), ("frozen", frozen_h, frozen),
    )):
        loads[name] = pltpu.make_async_copy(src, dst, load_sem.at[n])
    for name in ("og", "up", "acts", "down"):
        loads[name].start()

    x_peer = [lax.rem(x + d, F) for d in range(F)]
    x_from = [lax.rem(x + F - d, F) for d in range(F)]
    y_peer = [lax.rem(yi + d, I) for d in range(I)]
    y_from = [lax.rem(yi + I - d, I) for d in range(I)]
    z_peer = [lax.rem(zi + d, O) for d in range(O)]
    z_from = [lax.rem(zi + O - d, O) for d in range(O)]

    def x_id(d):
        return {"fsdp": x_peer[d]}

    def y_id(d):
        return {"dp": zi * I + y_peer[d]}

    def z_id(d):
        return {"dp": z_peer[d] * I + yi}

    core_id = {"section": 1 - core}
    others = (
        [x_id(d) for d in range(1, F)] + [y_id(d) for d in range(1, I)]
        + [z_id(d) for d in range(1, O)] + [core_id]
    )
    barrier = pltpu.get_barrier_semaphore()
    for other in others:
        pl.semaphore_signal(barrier, inc=1, device_id=other, device_id_type=MESH)

    sent = []

    def send(src, dst, ssem, rsem, to):
        copy = pltpu.make_async_remote_copy(
            src_ref=src, dst_ref=dst, send_sem=ssem, recv_sem=rsem, device_id=to, device_id_type=MESH
        )
        copy.start()
        sent.append(copy)

    def arrive(src, dst, ssem, rsem, to):
        pltpu.make_async_remote_copy(
            src_ref=src, dst_ref=dst, send_sem=ssem, recv_sem=rsem, device_id=to, device_id_type=MESH
        ).wait_recv()

    def proj_exchange(n, value):
        proj_send[n] = value.astype(BF16)
        for d in range(1, F):
            send(proj_send.at[n], proj_recv.at[n, d], x_send_sem.at[n, d], x_recv_sem.at[n, d], x_id(d))

    def proj_sum(n, value):
        for d in range(1, F):
            arrive(proj_send.at[n], proj_recv.at[n, d], x_send_sem.at[n, d], x_recv_sem.at[n, d], x_id(d))
            value = value + proj_recv[n, d].astype(F32)
        return value

    loads["og"].wait()
    loads["up"].wait()
    loads["prompts"].start()
    loads["frozen"].start()
    slot = T // lengths.shape[0]
    position = lax.broadcasted_iota(jnp.int32, (slot, C), 0)
    for i in range(lengths.shape[0]):
        weight = jnp.where(position < lengths[i], buckets[i].astype(F32) - 1.5, 0.0)
        block = og[i * slot:(i + 1) * slot, :].astype(F32)
        gk[x, i * slot:(i + 1) * slot, :] = (weight * block).astype(BF16)
    mine = gk[x]
    up_part = lax.dot_general(mine, up[...].astype(BF16), NT, preferred_element_type=F32)
    pl.semaphore_wait(barrier, len(others))
    proj_exchange(0, up_part)

    loads["acts"].wait()
    loads["down"].wait()
    a_half[...] = down[...].astype(BF16)
    down_part = jnp.dot(acts[...], a_half[...], preferred_element_type=F32)
    proj_exchange(1, down_part)

    loads["prompts"].wait()
    loads["frozen"].wait()
    tile_c = min(256, C)

    def frozen_part(owner, put, first=0, last=C // tile_c):
        @pl.loop(first, last)
        def _(t):
            cols = pl.ds(pl.multiple_of(t * tile_c, tile_c), tile_c)
            src = pl.ds(pl.multiple_of(owner * C + t * tile_c, tile_c), tile_c)
            put(cols, jnp.dot(prompts[...], frozen[:, src], preferred_element_type=F32))

    for d in range(1, F):
        def put_other(cols, value, d=d):
            kp_send[d, :, cols] = value.astype(BF16)

        frozen_part(x_peer[d], put_other)

    up_half = proj_sum(0, up_part)
    for d in range(1, F):
        send(gk.at[x], gk.at[x], x_send_sem.at[2, d], x_recv_sem.at[2, d], x_id(d))
    up_half_t = up_half.T.astype(BF16)
    up_half = up_half.astype(BF16)
    down_half_t = None

    def core_copy(k):
        return (gbuf.at[k, 1 - core], core_recv.at[k], d_send_sem.at[k, 0], d_recv_sem.at[k, 0], core_id)

    for k in range(K):
        for s in range(S):
            for i in range(I):
                n = (k * S + s) * I + i
                if n < plan.down_units:
                    part = jnp.dot(up_half_t, acts[:, n * U:(n + 1) * U], preferred_element_type=F32)
                elif n < plan.units:
                    if down_half_t is None:
                        down_half_t = proj_sum(1, down_part).T.astype(BF16)
                    m = n - plan.down_units
                    part = jnp.dot(down_half_t, gk[x, :, m * U:(m + 1) * U], preferred_element_type=F32)
                else:
                    part = jnp.zeros((plan.rank, U), F32)
                gbuf[k, s, i] = ADAPTER_SCALE * part
        send(*core_copy(k))
    for d in range(1, F):
        send(kp_send.at[d], kp_recv.at[d], x_send_sem.at[3, d], x_recv_sem.at[3, d], x_id(d))

    def y_copy(k, d):
        return (y_send.at[k, d], y_recv.at[k, d], d_send_sem.at[k, d], d_recv_sem.at[k, d], y_id(d))

    def z_copy(k, d):
        e = I + d
        return (z_send.at[k, z_peer[d]], z_recv.at[k, d], d_send_sem.at[k, e], d_recv_sem.at[k, e], z_id(d))

    for k in range(K):
        arrive(*core_copy(k))
        for d in range(I):
            value = gbuf[k, core, y_peer[d]] + core_recv[k, y_peer[d]]
            if d == 0:
                quarter[k] = value
            else:
                y_send[k, d] = value.astype(BF16)
                send(*y_copy(k, d))

    def put_own(cols, value):
        kp_own[:, cols] = value

    pd[...] = jnp.dot(prompts[...], a_half[...], preferred_element_type=F32)

    part_rows = plan.rank // O
    tiles_c = C // tile_c
    for k in range(K):
        value = quarter[k]
        for d in range(1, I):
            arrive(*y_copy(k, d))
            value = value + y_recv[k, d].astype(F32)
        quarter[k] = value
        for o in range(O):
            z_send[k, o] = value[o * part_rows:(o + 1) * part_rows].astype(BF16)
        for d in range(1, O):
            send(*z_copy(k, d))
        first, last = k * tiles_c // K, (k + 1) * tiles_c // K
        if first < last:
            frozen_part(x, put_own, first, last)

    base = I + O

    def ag_z(k, d, slot):
        e = base + d
        return (ag.at[k, core, yi, zi], ag.at[k, core, yi, slot], d_send_sem.at[k, e], d_recv_sem.at[k, e], z_id(d))

    def ag_y(k, d, slot):
        e = base + O + d
        return (ag.at[k, core, yi], ag.at[k, core, slot], d_send_sem.at[k, e], d_recv_sem.at[k, e], y_id(d))

    def ag_core(k, slot):
        e = base + O + I
        return (ag.at[k, core], ag.at[k, slot], d_send_sem.at[k, e], d_recv_sem.at[k, e], core_id)

    squares = jnp.zeros((part_rows, U), F32)
    for k in range(K):
        value = quarter[k, pl.ds(pl.multiple_of(zi * part_rows, part_rows), part_rows), :]
        for d in range(1, O):
            arrive(*z_copy(k, d))
            value = value + z_recv[k, d].astype(F32)
        rounded = value.astype(BF16)
        ag[k, core, yi, zi] = rounded
        for d in range(1, O):
            send(*ag_z(k, d, zi))
        value = rounded.astype(F32)
        squares = squares + value * value

    def sq_send(stage, value, own, count, to):
        sq[stage, own] = value
        for d in range(1, count):
            send(sq.at[stage, own], sq.at[stage, own], q_send_sem.at[stage, d], q_recv_sem.at[stage, d], to(d))

    def sq_sum(stage, own, count, to, source):
        for d in range(1, count):
            arrive(sq.at[stage, own], sq.at[stage, source(d)], q_send_sem.at[stage, d], q_recv_sem.at[stage, d], to(d))
        total = sq[stage, 0]
        for n in range(1, count):
            total = total + sq[stage, n]
        return total

    total = jnp.broadcast_to(jnp.sum(squares, keepdims=True), (8, 128))
    sq_send(0, total, zi, O, z_id)

    for k in range(K):
        for d in range(1, O):
            arrive(*ag_z(k, d, z_from[d]))
        for d in range(1, I):
            send(*ag_y(k, d, yi))
    total = sq_sum(0, zi, O, z_id, lambda d: z_from[d])
    sq_send(1, total, yi, I, y_id)

    for d in range(1, F):
        arrive(gk.at[x], gk.at[x_from[d]], x_send_sem.at[2, d], x_recv_sem.at[2, d], x_id(d))
    tile = plan.tile

    def ig_tile(t):
        span = pl.ds(pl.multiple_of(t * tile, tile), tile)
        value = ADAPTER_SCALE * lax.dot_general(up_half, a_half[span, :], NT, preferred_element_type=F32)
        for p in range(F):
            value = value + lax.dot_general(
                gk[p], frozen[span, p * C:(p + 1) * C], NT, preferred_element_type=F32
            )
        ig[:, span] = value.astype(BF16)

    tiles = W // tile
    for k in range(K):
        first, last = k * tiles // K, (k + 1) * tiles // K
        if first < last:
            pl.loop(first, last)(ig_tile)
        for d in range(1, I):
            arrive(*ag_y(k, d, y_from[d]))
        send(*ag_core(k, core))
    ig_store = pltpu.make_async_copy(ig, ig_h, store_sem.at[0])
    ig_store.start()
    total = sq_sum(1, yi, I, y_id, lambda d: y_from[d])
    sq_send(2, total, core, S, lambda d: core_id)
    total = sq_sum(2, core, S, lambda d: core_id, lambda d: 1 - core)
    sq_send(3, total, x, F, x_id)

    def unit_of(n):
        k, s, i = n // (S * I), (n // I) % S, n % I
        return ag[k, s, i].reshape(plan.rank, U)

    low = jnp.zeros((T, plan.rank), F32)
    for k in range(K):
        arrive(*ag_core(k, 1 - core))
        for n in range(k * S * I, (k + 1) * S * I):
            if n < plan.down_units:
                low = low + lax.dot_general(
                    prompts[:, n * U:(n + 1) * U], unit_of(n), NT, preferred_element_type=F32
                )
    total = sq_sum(3, x, F, x_id, lambda d: x_from[d])
    norm = jnp.sqrt(total + 1e-12)
    factor = (STEP_RATE * jnp.minimum(1.0, CLIP_NORM / norm))[0:1, 0:1]

    pg[...] = pd[...] - factor * low
    proj_exchange(2, pg[...])

    for n in range(plan.units):
        if n < plan.down_units:
            span = slice(n * U, (n + 1) * U)
            nd[span, :] = down[span, :] - factor * unit_of(n).astype(F32).T
        else:
            span = slice((n - plan.down_units) * U, (n - plan.down_units + 1) * U)
            nu[:, span] = up[:, span] - factor * unit_of(n).astype(F32)
    nd_store = pltpu.make_async_copy(nd, nd_h, store_sem.at[1])
    nd_store.start()
    nu_store = pltpu.make_async_copy(nu, nu_h, store_sem.at[2])
    nu_store.start()

    for d in range(1, F):
        arrive(kp_send.at[d], kp_recv.at[d], x_send_sem.at[3, d], x_recv_sem.at[3, d], x_id(d))
        kp_own[...] = kp_own[...] + kp_recv[d].astype(F32)
    low_half = (ADAPTER_SCALE * proj_sum(2, pg[...])).astype(BF16)
    keys[...] = (
        kp_own[...] + jnp.dot(low_half, nu[...].astype(BF16), preferred_element_type=F32)
    ).astype(BF16)
    keys_store = pltpu.make_async_copy(keys, keys_h, store_sem.at[3])
    keys_store.start()

    for copy in sent:
        copy.wait_send()
    ig_store.wait()
    nd_store.wait()
    nu_store.wait()
    keys_store.wait()


def move_kernel(pieces, *refs):
    sem = refs[-1]
    copies = []
    for n, (which, row, count) in enumerate(pieces):
        src, dst = refs[which], refs[4 + which]
        span = pl.ds(row, count)
        copies.append(pltpu.make_async_copy(src.at[span, :], dst.at[span, :], sem.at[n]))
        copies[-1].start()
    for copy in copies:
        copy.wait()


def per_device(mesh, acts, output_gradient, lengths, buckets, frozen, down, up, prompts):
    T, W = acts.shape
    C = output_gradient.shape[1]
    R = down.shape[1]
    plan = Plan(mesh, T, W, C, R)
    F, S, I, O, K, U = plan.fsdp, plan.cores, plan.inner, plan.outer, plan.chunks, plan.unit
    N = C * F
    smem = pl.BlockSpec(memory_space=pltpu.SMEM)
    hbm = pl.BlockSpec(memory_space=pl.ANY)
    dma = pltpu.SemaphoreType.DMA
    hops = I + O + O + I + 1
    scratch = [
        pltpu.VMEM((T, W), BF16), pltpu.VMEM((T, C), BF16), pltpu.VMEM((W, N), BF16),
        pltpu.VMEM((W, R), F32), pltpu.VMEM((R, C), F32), pltpu.VMEM((T, W), BF16),
        pltpu.VMEM((W, R), BF16), pltpu.VMEM((F, T, C), BF16),
        pltpu.VMEM((3, T, R), BF16), pltpu.VMEM((3, F, T, R), BF16),
        pltpu.VMEM((T, R), F32), pltpu.VMEM((T, R), F32),
        pltpu.VMEM((T, C), F32), pltpu.VMEM((F, T, C), BF16), pltpu.VMEM((F, T, C), BF16),
        pltpu.VMEM((K, S, I, R, U), F32), pltpu.VMEM((K, I, R, U), F32),
        pltpu.VMEM((K, I, R, U), BF16), pltpu.VMEM((K, I, R, U), BF16),
        pltpu.VMEM((K, R, U), F32),
        pltpu.VMEM((K, O, R // O, U), BF16), pltpu.VMEM((K, O, R // O, U), BF16),
        pltpu.VMEM((K, S, I, O, R // O, U), BF16),
        pltpu.VMEM((4, max(O, I, S, F), 8, 128), F32),
        pltpu.VMEM((T, W), BF16), pltpu.VMEM((W, R), F32), pltpu.VMEM((R, C), F32), pltpu.VMEM((T, C), BF16),
        dma((6,)), dma((4,)), dma((4, F)), dma((4, F)), dma((K, hops)), dma((K, hops)),
        dma((4, max(O, I, S, F))), dma((4, max(O, I, S, F))),
    ]
    results = pl.pallas_call(
        functools.partial(kernel, plan),
        out_shape=(
            jax.ShapeDtypeStruct((T, W), BF16),
            jax.ShapeDtypeStruct((W, R), F32),
            jax.ShapeDtypeStruct((R, C), F32),
            jax.ShapeDtypeStruct((T, C), BF16),
        ),
        in_specs=[smem, smem] + [hbm] * 6,
        out_specs=(hbm,) * 4,
        scratch_shapes=scratch,
        compiler_params=pltpu.CompilerParams(
            collective_id=0, has_side_effects=True, vmem_limit_bytes=60 * 1024 * 1024
        ),
        cost_estimate=pl.CostEstimate(
            flops=2 * T * W * (2 * N + 4 * R), bytes_accessed=2 * (3 * T * W + W * N), transcendentals=0
        ),
        name="adapter_step",
    )(lengths, buckets, acts, output_gradient, frozen, down, up, prompts)
    pieces = [(0, n * T // 4, T // 4) for n in range(4)] + [
        (1, n * W // 2, W // 2) for n in range(2)
    ] + [(2, 0, R), (3, 0, T)]
    return pl.pallas_call(
        functools.partial(move_kernel, pieces),
        out_shape=[jax.ShapeDtypeStruct(r.shape, r.dtype) for r in results],
        in_specs=[hbm] * 4,
        out_specs=[hbm] * 4,
        scratch_shapes=[dma((len(pieces),))],
        compiler_params=pltpu.CompilerParams(vmem_limit_bytes=60 * 1024 * 1024),
        name="move_results",
    )(*results)


def solution(mesh):
    tokens = P(("dp", "section"), "fsdp")
    return jax.shard_map(
        functools.partial(per_device, mesh),
        mesh=mesh,
        in_specs=(
            tokens, tokens, P(("dp", "section")), P(("dp", "section")),
            P("fsdp", None), P("fsdp", None), P(None, "fsdp"), tokens,
        ),
        out_specs=(tokens, P("fsdp", None), P(None, "fsdp"), tokens),
        check_vma=False,
    )
```

```python
import functools

import jax
import jax.numpy as jnp
from jax import lax
from jax.experimental import pallas as pl
from jax.experimental.pallas import tpu as pltpu
from jax.sharding import PartitionSpec as P

ADAPTER_SCALE = 0.5
STEP_RATE = 16.0
CLIP_NORM = 1.0
MESH = pl.DeviceIdType.MESH
F32 = jnp.float32
BF16 = jnp.bfloat16
NT = (((1,), (1,)), ((), ()))


class Plan:
    def __init__(self, mesh, rows, width, channels, rank):
        self.fsdp = mesh.shape["fsdp"]
        self.cores = mesh.shape["section"]
        dp = mesh.shape["dp"]
        self.outer = 4 if dp % 4 == 0 else 1
        self.inner = dp // self.outer
        self.rows, self.width, self.channels, self.rank = rows, width, channels, rank
        span = self.cores * self.inner
        self.unit = 256 if width % 256 == 0 and channels % 256 == 0 else 128
        units = (width + channels) // self.unit
        self.chunks = -(-units // span)
        self.down_units = width // self.unit
        self.units = units
        self.tile = 256 if width % 256 == 0 else 128


def kernel(
    plan,
    lengths, buckets, acts_h, og_h, frozen_h, down_h, up_h, prompts_h,
    ig, nd, nu, keys,
    acts, og, frozen, down, up, prompts,
    a_half, gk, proj_send, proj_recv, pd, pg,
    kp_own, kp_send, kp_recv,
    gbuf, core_recv, y_send, y_recv, quarter, z_send, z_recv, ag, sq,
    load_sem, x_send_sem, x_recv_sem, d_send_sem, d_recv_sem, q_send_sem, q_recv_sem,
):
    F, S, I, O, K = plan.fsdp, plan.cores, plan.inner, plan.outer, plan.chunks
    U, W, C = plan.unit, plan.width, plan.channels
    T = plan.rows
    x = lax.axis_index("fsdp")
    dp = lax.axis_index("dp")
    core = lax.axis_index("section")
    zi, yi = dp // I, dp % I

    loads = {}
    for n, (name, src, dst) in enumerate((
        ("og", og_h, og), ("up", up_h, up), ("acts", acts_h, acts), ("down", down_h, down),
        ("prompts", prompts_h, prompts), ("frozen", frozen_h, frozen),
    )):
        loads[name] = pltpu.make_async_copy(src, dst, load_sem.at[n])
    for name in ("og", "up", "acts", "down"):
        loads[name].start()

    x_peer = [lax.rem(x + d, F) for d in range(F)]
    x_from = [lax.rem(x + F - d, F) for d in range(F)]
    y_peer = [lax.rem(yi + d, I) for d in range(I)]
    y_from = [lax.rem(yi + I - d, I) for d in range(I)]
    z_peer = [lax.rem(zi + d, O) for d in range(O)]
    z_from = [lax.rem(zi + O - d, O) for d in range(O)]

    def x_id(d):
        return {"fsdp": x_peer[d]}

    def y_id(d):
        return {"dp": zi * I + y_peer[d]}

    def z_id(d):
        return {"dp": z_peer[d] * I + yi}

    core_id = {"section": 1 - core}
    others = (
        [x_id(d) for d in range(1, F)] + [y_id(d) for d in range(1, I)]
        + [z_id(d) for d in range(1, O)] + [core_id]
    )
    barrier = pltpu.get_barrier_semaphore()
    for other in others:
        pl.semaphore_signal(barrier, inc=1, device_id=other, device_id_type=MESH)

    sent = []

    def send(src, dst, ssem, rsem, to):
        copy = pltpu.make_async_remote_copy(
            src_ref=src, dst_ref=dst, send_sem=ssem, recv_sem=rsem, device_id=to, device_id_type=MESH
        )
        copy.start()
        sent.append(copy)

    def arrive(src, dst, ssem, rsem, to):
        pltpu.make_async_remote_copy(
            src_ref=src, dst_ref=dst, send_sem=ssem, recv_sem=rsem, device_id=to, device_id_type=MESH
        ).wait_recv()

    def proj_exchange(n, value):
        proj_send[n] = value.astype(BF16)
        for d in range(1, F):
            send(proj_send.at[n], proj_recv.at[n, d], x_send_sem.at[n, d], x_recv_sem.at[n, d], x_id(d))

    def proj_sum(n, value):
        for d in range(1, F):
            arrive(proj_send.at[n], proj_recv.at[n, d], x_send_sem.at[n, d], x_recv_sem.at[n, d], x_id(d))
            value = value + proj_recv[n, d].astype(F32)
        return value

    loads["og"].wait()
    loads["up"].wait()
    loads["prompts"].start()
    loads["frozen"].start()
    slot = T // lengths.shape[0]
    position = lax.broadcasted_iota(jnp.int32, (slot, C), 0)
    for i in range(lengths.shape[0]):
        weight = jnp.where(position < lengths[i], buckets[i].astype(F32) - 1.5, 0.0)
        block = og[i * slot:(i + 1) * slot, :].astype(F32)
        gk[x, i * slot:(i + 1) * slot, :] = (weight * block).astype(BF16)
    mine = gk[x]
    up_part = lax.dot_general(mine, up[...].astype(BF16), NT, preferred_element_type=F32)
    pl.semaphore_wait(barrier, len(others))
    proj_exchange(0, up_part)

    loads["acts"].wait()
    loads["down"].wait()
    a_half[...] = down[...].astype(BF16)
    down_part = jnp.dot(acts[...], a_half[...], preferred_element_type=F32)
    proj_exchange(1, down_part)

    loads["prompts"].wait()
    pd[...] = jnp.dot(prompts[...], a_half[...], preferred_element_type=F32)
    tile_c = min(256, C)

    def frozen_part(owner, put, first=0, last=C // tile_c):
        @pl.loop(first, last)
        def _(t):
            cols = pl.ds(pl.multiple_of(t * tile_c, tile_c), tile_c)
            src = pl.ds(pl.multiple_of(owner * C + t * tile_c, tile_c), tile_c)
            put(cols, jnp.dot(prompts[...], frozen[:, src], preferred_element_type=F32))

    up_half = proj_sum(0, up_part)
    for d in range(1, F):
        send(gk.at[x], gk.at[x], x_send_sem.at[2, d], x_recv_sem.at[2, d], x_id(d))
    up_half_t = up_half.T.astype(BF16)
    up_half = up_half.astype(BF16)
    down_half_t = None

    def core_copy(k):
        return (gbuf.at[k, 1 - core], core_recv.at[k], d_send_sem.at[k, 0], d_recv_sem.at[k, 0], core_id)

    for k in range(K):
        for s in range(S):
            for i in range(I):
                n = (k * S + s) * I + i
                if n < plan.down_units:
                    part = jnp.dot(up_half_t, acts[:, n * U:(n + 1) * U], preferred_element_type=F32)
                elif n < plan.units:
                    if down_half_t is None:
                        down_half_t = proj_sum(1, down_part).T.astype(BF16)
                    m = n - plan.down_units
                    part = jnp.dot(down_half_t, gk[x, :, m * U:(m + 1) * U], preferred_element_type=F32)
                else:
                    part = jnp.zeros((plan.rank, U), F32)
                gbuf[k, s, i] = ADAPTER_SCALE * part
        send(*core_copy(k))
    def y_copy(k, d):
        return (y_send.at[k, d], y_recv.at[k, d], d_send_sem.at[k, d], d_recv_sem.at[k, d], y_id(d))

    def z_copy(k, d):
        e = I + d
        return (z_send.at[k, z_peer[d]], z_recv.at[k, d], d_send_sem.at[k, e], d_recv_sem.at[k, e], z_id(d))

    for k in range(K):
        arrive(*core_copy(k))
        for d in range(I):
            value = gbuf[k, core, y_peer[d]] + core_recv[k, y_peer[d]]
            if d == 0:
                quarter[k] = value
            else:
                y_send[k, d] = value.astype(BF16)
                send(*y_copy(k, d))

    def put_own(cols, value):
        kp_own[:, cols] = value

    loads["frozen"].wait()
    part_rows = plan.rank // O
    tiles_c = C // tile_c

    def share(n, step):
        return step * n // K, (step + 1) * n // K

    for k in range(K):
        first, last = share(tiles_c, K - 1 - k)
        for d in range(1, F):
            def put_other(cols, value, d=d):
                kp_send[d, :, cols] = value.astype(BF16)

            if first < last:
                frozen_part(x_peer[d], put_other, first, last)
        value = quarter[k]
        for d in range(1, I):
            arrive(*y_copy(k, d))
            value = value + y_recv[k, d].astype(F32)
        quarter[k] = value
        for o in range(O):
            z_send[k, o] = value[o * part_rows:(o + 1) * part_rows].astype(BF16)
        for d in range(1, O):
            send(*z_copy(k, d))
    for d in range(1, F):
        send(kp_send.at[d], kp_recv.at[d], x_send_sem.at[3, d], x_recv_sem.at[3, d], x_id(d))

    base = I + O

    def ag_z(k, d, slot):
        e = base + d
        return (ag.at[k, core, yi, zi], ag.at[k, core, yi, slot], d_send_sem.at[k, e], d_recv_sem.at[k, e], z_id(d))

    def ag_y(k, d, slot):
        e = base + O + d
        return (ag.at[k, core, yi], ag.at[k, core, slot], d_send_sem.at[k, e], d_recv_sem.at[k, e], y_id(d))

    def ag_core(k, slot):
        e = base + O + I
        return (ag.at[k, core], ag.at[k, slot], d_send_sem.at[k, e], d_recv_sem.at[k, e], core_id)

    squares = jnp.zeros((part_rows, U), F32)
    for k in range(K):
        first, last = share(tiles_c, K - 1 - k)
        if first < last:
            frozen_part(x, put_own, first, last)
        value = quarter[k, pl.ds(pl.multiple_of(zi * part_rows, part_rows), part_rows), :]
        for d in range(1, O):
            arrive(*z_copy(k, d))
            value = value + z_recv[k, d].astype(F32)
        rounded = value.astype(BF16)
        ag[k, core, yi, zi] = rounded
        for d in range(1, O):
            send(*ag_z(k, d, zi))
        value = rounded.astype(F32)
        squares = squares + value * value

    def sq_send(stage, value, own, count, to):
        sq[stage, own] = value
        for d in range(1, count):
            send(sq.at[stage, own], sq.at[stage, own], q_send_sem.at[stage, d], q_recv_sem.at[stage, d], to(d))

    def sq_sum(stage, own, count, to, source):
        for d in range(1, count):
            arrive(sq.at[stage, own], sq.at[stage, source(d)], q_send_sem.at[stage, d], q_recv_sem.at[stage, d], to(d))
        total = sq[stage, 0]
        for n in range(1, count):
            total = total + sq[stage, n]
        return total

    total = jnp.broadcast_to(jnp.sum(squares, keepdims=True), (8, 128))
    sq_send(0, total, zi, O, z_id)

    for k in range(K):
        for d in range(1, O):
            arrive(*ag_z(k, d, z_from[d]))
        for d in range(1, I):
            send(*ag_y(k, d, yi))
    total = sq_sum(0, zi, O, z_id, lambda d: z_from[d])
    sq_send(1, total, yi, I, y_id)

    for d in range(1, F):
        arrive(gk.at[x], gk.at[x_from[d]], x_send_sem.at[2, d], x_recv_sem.at[2, d], x_id(d))
    tile = plan.tile

    def ig_tile(t):
        span = pl.ds(pl.multiple_of(t * tile, tile), tile)
        value = ADAPTER_SCALE * lax.dot_general(up_half, a_half[span, :], NT, preferred_element_type=F32)
        for p in range(F):
            value = value + lax.dot_general(
                gk[p], frozen[span, p * C:(p + 1) * C], NT, preferred_element_type=F32
            )
        ig[:, span] = value.astype(BF16)

    tiles = W // tile
    for k in range(K):
        first, last = share(tiles, k)
        if first < last:
            pl.loop(first, last)(ig_tile)
        for d in range(1, I):
            arrive(*ag_y(k, d, y_from[d]))
        send(*ag_core(k, core))
    total = sq_sum(1, yi, I, y_id, lambda d: y_from[d])
    sq_send(2, total, core, S, lambda d: core_id)
    total = sq_sum(2, core, S, lambda d: core_id, lambda d: 1 - core)
    sq_send(3, total, x, F, x_id)

    def unit_of(n):
        k, s, i = n // (S * I), (n // I) % S, n % I
        return ag[k, s, i].reshape(plan.rank, U)

    low = jnp.zeros((T, plan.rank), F32)
    for k in range(K):
        arrive(*ag_core(k, 1 - core))
        for n in range(k * S * I, (k + 1) * S * I):
            if n < plan.down_units:
                low = low + lax.dot_general(
                    prompts[:, n * U:(n + 1) * U], unit_of(n), NT, preferred_element_type=F32
                )
    total = sq_sum(3, x, F, x_id, lambda d: x_from[d])
    norm = jnp.sqrt(total + 1e-12)
    factor = (STEP_RATE * jnp.minimum(1.0, CLIP_NORM / norm))[0:1, 0:1]

    pg[...] = pd[...] - factor * low
    proj_exchange(2, pg[...])

    for n in range(plan.units):
        if n < plan.down_units:
            span = slice(n * U, (n + 1) * U)
            nd[span, :] = down[span, :] - factor * unit_of(n).astype(F32).T
        else:
            span = slice((n - plan.down_units) * U, (n - plan.down_units + 1) * U)
            nu[:, span] = up[:, span] - factor * unit_of(n).astype(F32)

    for d in range(1, F):
        arrive(kp_send.at[d], kp_recv.at[d], x_send_sem.at[3, d], x_recv_sem.at[3, d], x_id(d))
        kp_own[...] = kp_own[...] + kp_recv[d].astype(F32)
    low_half = (ADAPTER_SCALE * proj_sum(2, pg[...])).astype(BF16)
    keys[...] = (
        kp_own[...] + jnp.dot(low_half, nu[...].astype(BF16), preferred_element_type=F32)
    ).astype(BF16)

    for copy in sent:
        copy.wait_send()


def move_kernel(pieces, *refs):
    sem = refs[-1]
    copies = []
    for n, (which, row, count) in enumerate(pieces):
        src, dst = refs[which], refs[4 + which]
        span = pl.ds(row, count)
        copies.append(pltpu.make_async_copy(src.at[span, :], dst.at[span, :], sem.at[n]))
        copies[-1].start()
    for copy in copies:
        copy.wait()


def per_device(mesh, acts, output_gradient, lengths, buckets, frozen, down, up, prompts):
    T, W = acts.shape
    C = output_gradient.shape[1]
    R = down.shape[1]
    plan = Plan(mesh, T, W, C, R)
    F, S, I, O, K, U = plan.fsdp, plan.cores, plan.inner, plan.outer, plan.chunks, plan.unit
    N = C * F
    smem = pl.BlockSpec(memory_space=pltpu.SMEM)
    hbm = pl.BlockSpec(memory_space=pl.ANY)
    vmem = pl.BlockSpec(memory_space=pltpu.VMEM)
    dma = pltpu.SemaphoreType.DMA
    hops = I + O + O + I + 1
    scratch = [
        pltpu.VMEM((T, W), BF16), pltpu.VMEM((T, C), BF16), pltpu.VMEM((W, N), BF16),
        pltpu.VMEM((W, R), F32), pltpu.VMEM((R, C), F32), pltpu.VMEM((T, W), BF16),
        pltpu.VMEM((W, R), BF16), pltpu.VMEM((F, T, C), BF16),
        pltpu.VMEM((3, T, R), BF16), pltpu.VMEM((3, F, T, R), BF16),
        pltpu.VMEM((T, R), F32), pltpu.VMEM((T, R), F32),
        pltpu.VMEM((T, C), F32), pltpu.VMEM((F, T, C), BF16), pltpu.VMEM((F, T, C), BF16),
        pltpu.VMEM((K, S, I, R, U), F32), pltpu.VMEM((K, I, R, U), F32),
        pltpu.VMEM((K, I, R, U), BF16), pltpu.VMEM((K, I, R, U), BF16),
        pltpu.VMEM((K, R, U), F32),
        pltpu.VMEM((K, O, R // O, U), BF16), pltpu.VMEM((K, O, R // O, U), BF16),
        pltpu.VMEM((K, S, I, O, R // O, U), BF16),
        pltpu.VMEM((4, max(O, I, S, F), 8, 128), F32),
        dma((6,)), dma((4, F)), dma((4, F)), dma((K, hops)), dma((K, hops)),
        dma((4, max(O, I, S, F))), dma((4, max(O, I, S, F))),
    ]
    results = pl.pallas_call(
        functools.partial(kernel, plan),
        out_shape=(
            pltpu.VMEM((T, W), BF16), pltpu.VMEM((W, R), F32), pltpu.VMEM((R, C), F32), pltpu.VMEM((T, C), BF16),
        ),
        in_specs=[smem, smem] + [hbm] * 6,
        out_specs=(vmem,) * 4,
        scratch_shapes=scratch,
        compiler_params=pltpu.CompilerParams(
            collective_id=0, has_side_effects=True, vmem_limit_bytes=48 * 1024 * 1024
        ),
        cost_estimate=pl.CostEstimate(
            flops=2 * T * W * (2 * N + 4 * R), bytes_accessed=2 * (3 * T * W + W * N), transcendentals=0
        ),
        name="adapter_step",
    )(*(
        pltpu.with_memory_space_constraint(a, pltpu.HBM)
        for a in (lengths, buckets, acts, output_gradient, frozen, down, up, prompts)
    ))
    pieces = [(0, n * T // 4, T // 4) for n in range(4)] + [
        (1, n * W // 2, W // 2) for n in range(2)
    ] + [(2, 0, R), (3, 0, T)]
    return pl.pallas_call(
        functools.partial(move_kernel, pieces),
        out_shape=[pltpu.HBM(r.shape, r.dtype) for r in results],
        in_specs=[vmem] * 4,
        out_specs=[hbm] * 4,
        scratch_shapes=[dma((len(pieces),))],
        name="move_results",
    )(*results)


def solution(mesh):
    tokens = P(("dp", "section"), "fsdp")
    return jax.shard_map(
        functools.partial(per_device, mesh),
        mesh=mesh,
        in_specs=(
            tokens, tokens, P(("dp", "section")), P(("dp", "section")),
            P("fsdp", None), P("fsdp", None), P(None, "fsdp"), tokens,
        ),
        out_specs=(tokens, P("fsdp", None), P(None, "fsdp"), tokens),
        check_vma=False,
    )
```

```python
import functools

import jax
import jax.numpy as jnp
from jax import lax
from jax.experimental import pallas as pl
from jax.experimental.pallas import tpu as pltpu
from jax.sharding import PartitionSpec as P

ADAPTER_SCALE = 0.5
STEP_RATE = 16.0
CLIP_NORM = 1.0
MESH = pl.DeviceIdType.MESH
F32 = jnp.float32
BF16 = jnp.bfloat16
NT = (((1,), (1,)), ((), ()))


class Plan:
    def __init__(self, mesh, rows, width, channels, rank):
        self.fsdp = mesh.shape["fsdp"]
        self.cores = mesh.shape["section"]
        dp = mesh.shape["dp"]
        self.outer = 4 if dp % 4 == 0 else 1
        self.inner = dp // self.outer
        self.rows, self.width, self.channels, self.rank = rows, width, channels, rank
        span = self.cores * self.inner
        self.unit = 256 if width % 256 == 0 and channels % 256 == 0 else 128
        units = (width + channels) // self.unit
        self.chunks = -(-units // span)
        self.down_units = width // self.unit
        self.units = units
        self.tile = 256 if width % 256 == 0 else 128


def kernel(
    plan,
    lengths, buckets, acts_h, og_h, frozen_h, down_h, up_h, prompts_h,
    ig, nd, nu, keys,
    acts, og, frozen, down, up, prompts,
    a_half, gk, proj_send, proj_recv, pd, pg,
    kp_own, kp_send, kp_recv,
    gbuf, core_recv, y_send, y_recv, quarter, z_send, z_recv, ag, sq,
    load_sem, x_send_sem, x_recv_sem, d_send_sem, d_recv_sem, q_send_sem, q_recv_sem,
):
    F, S, I, O, K = plan.fsdp, plan.cores, plan.inner, plan.outer, plan.chunks
    U, W, C = plan.unit, plan.width, plan.channels
    T = plan.rows
    x = lax.axis_index("fsdp")
    dp = lax.axis_index("dp")
    core = lax.axis_index("section")
    zi, yi = dp // I, dp % I

    loads = {}
    for n, (name, src, dst) in enumerate((
        ("og", og_h, og), ("up", up_h, up), ("acts", acts_h, acts), ("down", down_h, down),
        ("prompts", prompts_h, prompts), ("frozen", frozen_h, frozen),
    )):
        loads[name] = pltpu.make_async_copy(src, dst, load_sem.at[n])
    for name in ("og", "up", "acts", "down"):
        loads[name].start()

    x_peer = [lax.rem(x + d, F) for d in range(F)]
    x_from = [lax.rem(x + F - d, F) for d in range(F)]
    y_peer = [lax.rem(yi + d, I) for d in range(I)]
    y_from = [lax.rem(yi + I - d, I) for d in range(I)]
    z_peer = [lax.rem(zi + d, O) for d in range(O)]
    z_from = [lax.rem(zi + O - d, O) for d in range(O)]

    def x_id(d):
        return {"fsdp": x_peer[d]}

    def y_id(d):
        return {"dp": zi * I + y_peer[d]}

    def z_id(d):
        return {"dp": z_peer[d] * I + yi}

    core_id = {"section": 1 - core}

    def dp_id(p):
        return {"dp": p}

    def group_id(p):
        return {"fsdp": p // S, "section": p % S}

    others = [dp_id(lax.rem(dp + d, O * I)) for d in range(1, O * I)] + [
        group_id(lax.rem(x * S + core + d, F * S)) for d in range(1, F * S)
    ]
    barrier = pltpu.get_barrier_semaphore()
    for other in others:
        pl.semaphore_signal(barrier, inc=1, device_id=other, device_id_type=MESH)

    sent = []

    def send(src, dst, ssem, rsem, to):
        copy = pltpu.make_async_remote_copy(
            src_ref=src, dst_ref=dst, send_sem=ssem, recv_sem=rsem, device_id=to, device_id_type=MESH
        )
        copy.start()
        sent.append(copy)

    def arrive(src, dst, ssem, rsem, to):
        pltpu.make_async_remote_copy(
            src_ref=src, dst_ref=dst, send_sem=ssem, recv_sem=rsem, device_id=to, device_id_type=MESH
        ).wait_recv()

    def proj_exchange(n, value):
        proj_send[n] = value.astype(BF16)
        for d in range(1, F):
            send(proj_send.at[n], proj_recv.at[n, d], x_send_sem.at[n, d], x_recv_sem.at[n, d], x_id(d))

    def proj_sum(n, value):
        for d in range(1, F):
            arrive(proj_send.at[n], proj_recv.at[n, d], x_send_sem.at[n, d], x_recv_sem.at[n, d], x_id(d))
            value = value + proj_recv[n, d].astype(F32)
        return value

    loads["og"].wait()
    loads["up"].wait()
    loads["prompts"].start()
    loads["frozen"].start()
    slot = T // lengths.shape[0]
    position = lax.broadcasted_iota(jnp.int32, (slot, C), 0)
    for i in range(lengths.shape[0]):
        weight = jnp.where(position < lengths[i], buckets[i].astype(F32) - 1.5, 0.0)
        block = og[i * slot:(i + 1) * slot, :].astype(F32)
        gk[x, i * slot:(i + 1) * slot, :] = (weight * block).astype(BF16)
    mine = gk[x]
    up_part = lax.dot_general(mine, up[...].astype(BF16), NT, preferred_element_type=F32)
    pl.semaphore_wait(barrier, len(others))
    proj_exchange(0, up_part)

    loads["acts"].wait()
    loads["down"].wait()
    a_half[...] = down[...].astype(BF16)
    down_part = jnp.dot(acts[...], a_half[...], preferred_element_type=F32)
    proj_exchange(1, down_part)

    loads["prompts"].wait()
    pd[...] = jnp.dot(prompts[...], a_half[...], preferred_element_type=F32)
    tile_c = min(256, C)

    def frozen_part(owner, put, first=0, last=C // tile_c):
        @pl.loop(first, last)
        def _(t):
            cols = pl.ds(pl.multiple_of(t * tile_c, tile_c), tile_c)
            src = pl.ds(pl.multiple_of(owner * C + t * tile_c, tile_c), tile_c)
            put(cols, jnp.dot(prompts[...], frozen[:, src], preferred_element_type=F32))

    up_half = proj_sum(0, up_part)
    up_half_t = up_half.T.astype(BF16)
    up_half = up_half.astype(BF16)
    down_half_t = None

    def core_copy(k):
        return (gbuf.at[k, 1 - core], core_recv.at[k], d_send_sem.at[k, 0], d_recv_sem.at[k, 0], core_id)

    for k in range(K):
        for s in range(S):
            for i in range(I):
                n = (k * S + s) * I + i
                if n < plan.down_units:
                    part = jnp.dot(up_half_t, acts[:, n * U:(n + 1) * U], preferred_element_type=F32)
                elif n < plan.units:
                    if down_half_t is None:
                        down_half_t = proj_sum(1, down_part).T.astype(BF16)
                        for d in range(1, F):
                            send(gk.at[x], gk.at[x], x_send_sem.at[4, d], x_recv_sem.at[4, d], x_id(d))
                    m = n - plan.down_units
                    part = jnp.dot(down_half_t, gk[x, :, m * U:(m + 1) * U], preferred_element_type=F32)
                else:
                    part = jnp.zeros((plan.rank, U), F32)
                gbuf[k, s, i] = ADAPTER_SCALE * part
        send(*core_copy(k))
    def y_copy(k, d):
        return (y_send.at[k, d], y_recv.at[k, d], d_send_sem.at[k, d], d_recv_sem.at[k, d], y_id(d))

    def z_copy(k, d):
        e = I + d
        return (z_send.at[k, z_peer[d]], z_recv.at[k, d], d_send_sem.at[k, e], d_recv_sem.at[k, e], z_id(d))

    for k in range(K):
        arrive(*core_copy(k))
        for d in range(I):
            value = gbuf[k, core, y_peer[d]] + core_recv[k, y_peer[d]]
            if d == 0:
                quarter[k] = value
            else:
                y_send[k, d] = value.astype(BF16)
                send(*y_copy(k, d))

    def put_own(cols, value):
        kp_own[:, cols] = value

    loads["frozen"].wait()
    part_rows = plan.rank // O
    tiles_c = C // tile_c

    def share(n, step):
        return step * n // K, (step + 1) * n // K

    for k in range(K):
        first, last = share(tiles_c, K - 1 - k)
        for d in range(1, F):
            def put_other(cols, value, d=d):
                kp_send[d, :, cols] = value.astype(BF16)

            if first < last:
                frozen_part(x_peer[d], put_other, first, last)
        value = quarter[k]
        for d in range(1, I):
            arrive(*y_copy(k, d))
            value = value + y_recv[k, d].astype(F32)
        quarter[k] = value
        for o in range(O):
            z_send[k, o] = value[o * part_rows:(o + 1) * part_rows].astype(BF16)
        for d in range(1, O):
            send(*z_copy(k, d))

    base = I + O

    def ag_z(k, d, slot):
        e = base + d
        return (ag.at[k, core, yi, zi], ag.at[k, core, yi, slot], d_send_sem.at[k, e], d_recv_sem.at[k, e], z_id(d))

    def ag_y(k, d, slot):
        e = base + O + d
        return (ag.at[k, core, yi], ag.at[k, core, slot], d_send_sem.at[k, e], d_recv_sem.at[k, e], y_id(d))

    def ag_core(k, slot):
        e = base + O + I
        return (ag.at[k, core], ag.at[k, slot], d_send_sem.at[k, e], d_recv_sem.at[k, e], core_id)

    squares = jnp.zeros((part_rows, U), F32)
    for k in range(K):
        first, last = share(tiles_c, K - 1 - k)
        if first < last:
            frozen_part(x, put_own, first, last)
        value = quarter[k, pl.ds(pl.multiple_of(zi * part_rows, part_rows), part_rows), :]
        for d in range(1, O):
            arrive(*z_copy(k, d))
            value = value + z_recv[k, d].astype(F32)
        rounded = value.astype(BF16)
        ag[k, core, yi, zi] = rounded
        for d in range(1, O):
            send(*ag_z(k, d, zi))
        value = rounded.astype(F32)
        squares = squares + value * value

    D, G = O * I, F * S
    dp_peer = [lax.rem(dp + d, D) for d in range(D)]
    group = x * S + core
    group_peer = [lax.rem(group + d, G) for d in range(G)]

    def sq_copy(stage, own, slot, d, to):
        return (sq.at[stage, own], sq.at[stage, slot], q_send_sem.at[stage, d], q_recv_sem.at[stage, d], to)

    def sq_send(stage, value, own, peers, to):
        sq[stage, own] = value
        for d in range(1, len(peers)):
            send(*sq_copy(stage, own, own, d, to(peers[d])))

    def sq_sum(stage, own, peers, to):
        count = len(peers)
        for d in range(1, count):
            arrive(*sq_copy(stage, own, lax.rem(own + count - d, count), d, to(peers[d])))
        total = sq[stage, 0]
        for n in range(1, count):
            total = total + sq[stage, n]
        return total

    total = jnp.broadcast_to(jnp.sum(squares, keepdims=True), (8, 128))
    sq_send(0, total, dp, dp_peer, dp_id)

    for k in range(K):
        for d in range(1, O):
            arrive(*ag_z(k, d, z_from[d]))
        for d in range(1, I):
            send(*ag_y(k, d, yi))
    sq_send(1, sq_sum(0, dp, dp_peer, dp_id), group, group_peer, group_id)

    for d in range(1, F):
        arrive(gk.at[x], gk.at[x_from[d]], x_send_sem.at[4, d], x_recv_sem.at[4, d], x_id(d))
    for d in range(1, F):
        send(kp_send.at[d], kp_recv.at[d], x_send_sem.at[3, d], x_recv_sem.at[3, d], x_id(d))
    tile = plan.tile

    def ig_tile(t):
        span = pl.ds(pl.multiple_of(t * tile, tile), tile)
        value = ADAPTER_SCALE * lax.dot_general(up_half, a_half[span, :], NT, preferred_element_type=F32)
        for p in range(F):
            value = value + lax.dot_general(
                gk[p], frozen[span, p * C:(p + 1) * C], NT, preferred_element_type=F32
            )
        ig[:, span] = value.astype(BF16)

    tiles = W // tile
    for k in range(K):
        first, last = share(tiles, k)
        if first < last:
            pl.loop(first, last)(ig_tile)
        for d in range(1, I):
            arrive(*ag_y(k, d, y_from[d]))
        send(*ag_core(k, core))

    def unit_of(n):
        k, s, i = n // (S * I), (n // I) % S, n % I
        return ag[k, s, i].reshape(plan.rank, U)

    low = jnp.zeros((T, plan.rank), F32)
    for k in range(K):
        arrive(*ag_core(k, 1 - core))
        for n in range(k * S * I, (k + 1) * S * I):
            if n < plan.down_units:
                low = low + lax.dot_general(
                    prompts[:, n * U:(n + 1) * U], unit_of(n), NT, preferred_element_type=F32
                )
    total = sq_sum(1, group, group_peer, group_id)
    norm = jnp.sqrt(total + 1e-12)
    factor = (STEP_RATE * jnp.minimum(1.0, CLIP_NORM / norm))[0:1, 0:1]

    pg[...] = pd[...] - factor * low
    proj_exchange(2, pg[...])

    for n in range(plan.units):
        if n < plan.down_units:
            span = slice(n * U, (n + 1) * U)
            nd[span, :] = down[span, :] - factor * unit_of(n).astype(F32).T
        else:
            span = slice((n - plan.down_units) * U, (n - plan.down_units + 1) * U)
            nu[:, span] = up[:, span] - factor * unit_of(n).astype(F32)

    for d in range(1, F):
        arrive(kp_send.at[d], kp_recv.at[d], x_send_sem.at[3, d], x_recv_sem.at[3, d], x_id(d))
        kp_own[...] = kp_own[...] + kp_recv[d].astype(F32)
    low_half = (ADAPTER_SCALE * proj_sum(2, pg[...])).astype(BF16)
    keys[...] = (
        kp_own[...] + jnp.dot(low_half, nu[...].astype(BF16), preferred_element_type=F32)
    ).astype(BF16)

    for copy in sent:
        copy.wait_send()


def move_kernel(pieces, *refs):
    sem = refs[-1]
    copies = []
    for n, (which, row, count) in enumerate(pieces):
        src, dst = refs[which], refs[4 + which]
        span = pl.ds(row, count)
        copies.append(pltpu.make_async_copy(src.at[span, :], dst.at[span, :], sem.at[n]))
        copies[-1].start()
    for copy in copies:
        copy.wait()


def per_device(mesh, acts, output_gradient, lengths, buckets, frozen, down, up, prompts):
    T, W = acts.shape
    C = output_gradient.shape[1]
    R = down.shape[1]
    plan = Plan(mesh, T, W, C, R)
    F, S, I, O, K, U = plan.fsdp, plan.cores, plan.inner, plan.outer, plan.chunks, plan.unit
    N = C * F
    smem = pl.BlockSpec(memory_space=pltpu.SMEM)
    hbm = pl.BlockSpec(memory_space=pl.ANY)
    vmem = pl.BlockSpec(memory_space=pltpu.VMEM)
    dma = pltpu.SemaphoreType.DMA
    hops = I + O + O + I + 1
    scratch = [
        pltpu.VMEM((T, W), BF16), pltpu.VMEM((T, C), BF16), pltpu.VMEM((W, N), BF16),
        pltpu.VMEM((W, R), F32), pltpu.VMEM((R, C), F32), pltpu.VMEM((T, W), BF16),
        pltpu.VMEM((W, R), BF16), pltpu.VMEM((F, T, C), BF16),
        pltpu.VMEM((3, T, R), BF16), pltpu.VMEM((3, F, T, R), BF16),
        pltpu.VMEM((T, R), F32), pltpu.VMEM((T, R), F32),
        pltpu.VMEM((T, C), F32), pltpu.VMEM((F, T, C), BF16), pltpu.VMEM((F, T, C), BF16),
        pltpu.VMEM((K, S, I, R, U), F32), pltpu.VMEM((K, I, R, U), F32),
        pltpu.VMEM((K, I, R, U), BF16), pltpu.VMEM((K, I, R, U), BF16),
        pltpu.VMEM((K, R, U), F32),
        pltpu.VMEM((K, O, R // O, U), BF16), pltpu.VMEM((K, O, R // O, U), BF16),
        pltpu.VMEM((K, S, I, O, R // O, U), BF16),
        pltpu.VMEM((2, max(O * I, F * S), 8, 128), F32),
        dma((6,)), dma((5, F)), dma((5, F)), dma((K, hops)), dma((K, hops)),
        dma((2, max(O * I, F * S))), dma((2, max(O * I, F * S))),
    ]
    results = pl.pallas_call(
        functools.partial(kernel, plan),
        out_shape=(
            pltpu.VMEM((T, W), BF16), pltpu.VMEM((W, R), F32), pltpu.VMEM((R, C), F32), pltpu.VMEM((T, C), BF16),
        ),
        in_specs=[smem, smem] + [hbm] * 6,
        out_specs=(vmem,) * 4,
        scratch_shapes=scratch,
        compiler_params=pltpu.CompilerParams(
            collective_id=0, has_side_effects=True, vmem_limit_bytes=48 * 1024 * 1024
        ),
        cost_estimate=pl.CostEstimate(
            flops=2 * T * W * (2 * N + 4 * R), bytes_accessed=2 * (3 * T * W + W * N), transcendentals=0
        ),
        name="adapter_step",
    )(*(
        pltpu.with_memory_space_constraint(a, pltpu.HBM)
        for a in (lengths, buckets, acts, output_gradient, frozen, down, up, prompts)
    ))
    pieces = [(0, n * T // 4, T // 4) for n in range(4)] + [
        (1, n * W // 2, W // 2) for n in range(2)
    ] + [(2, 0, R), (3, 0, T)]
    return pl.pallas_call(
        functools.partial(move_kernel, pieces),
        out_shape=[pltpu.HBM(r.shape, r.dtype) for r in results],
        in_specs=[vmem] * 4,
        out_specs=[hbm] * 4,
        scratch_shapes=[dma((len(pieces),))],
        compiler_params=pltpu.CompilerParams(vmem_limit_bytes=16 * 1024 * 1024),
        name="move_results",
    )(*(pltpu.with_memory_space_constraint(r, pltpu.VMEM) for r in results))


def solution(mesh):
    tokens = P(("dp", "section"), "fsdp")
    return jax.shard_map(
        functools.partial(per_device, mesh),
        mesh=mesh,
        in_specs=(
            tokens, tokens, P(("dp", "section")), P(("dp", "section")),
            P("fsdp", None), P("fsdp", None), P(None, "fsdp"), tokens,
        ),
        out_specs=(tokens, P("fsdp", None), P(None, "fsdp"), tokens),
        check_vma=False,
    )
```

```python
import functools

import jax
import jax.numpy as jnp
from jax import lax
from jax.experimental import pallas as pl
from jax.experimental.pallas import tpu as pltpu
from jax.sharding import PartitionSpec as P

ADAPTER_SCALE = 0.5
STEP_RATE = 16.0
CLIP_NORM = 1.0
MESH = pl.DeviceIdType.MESH
F32 = jnp.float32
BF16 = jnp.bfloat16
NT = (((1,), (1,)), ((), ()))


class Plan:
    def __init__(self, mesh, rows, width, channels, rank):
        self.fsdp = mesh.shape["fsdp"]
        self.cores = mesh.shape["section"]
        dp = mesh.shape["dp"]
        self.outer = 4 if dp % 4 == 0 else 1
        self.inner = dp // self.outer
        self.rows, self.width, self.channels, self.rank = rows, width, channels, rank
        span = self.cores * self.inner
        self.unit = 256 if width % 256 == 0 and channels % 256 == 0 else 128
        units = (width + channels) // self.unit
        self.chunks = -(-units // span)
        self.down_units = width // self.unit
        self.units = units
        self.tile = 256 if width % 256 == 0 else 128


def kernel(
    plan,
    lengths, buckets, acts_h, og_h, frozen_h, down_h, up_h, prompts_h,
    ig, nd, nu, keys,
    acts, og, frozen, down, up, prompts,
    a_half, gk, proj_send, proj_recv, pd, pg,
    kp_own, kp_send, kp_recv,
    gbuf, core_recv, y_send, y_recv, quarter, z_send, z_recv, ag, sq,
    load_sem, x_send_sem, x_recv_sem, d_send_sem, d_recv_sem, q_send_sem, q_recv_sem,
):
    F, S, I, O, K = plan.fsdp, plan.cores, plan.inner, plan.outer, plan.chunks
    U, W, C = plan.unit, plan.width, plan.channels
    T = plan.rows
    x = lax.axis_index("fsdp")
    dp = lax.axis_index("dp")
    core = lax.axis_index("section")
    zi, yi = dp // I, dp % I

    loads = {}
    for n, (name, src, dst) in enumerate((
        ("og", og_h, og), ("up", up_h, up), ("acts", acts_h, acts), ("down", down_h, down),
        ("prompts", prompts_h, prompts), ("frozen", frozen_h, frozen),
    )):
        loads[name] = pltpu.make_async_copy(src, dst, load_sem.at[n])
    for name in ("og", "up", "acts", "down"):
        loads[name].start()

    x_peer = [lax.rem(x + d, F) for d in range(F)]
    x_from = [lax.rem(x + F - d, F) for d in range(F)]
    y_peer = [lax.rem(yi + d, I) for d in range(I)]
    y_from = [lax.rem(yi + I - d, I) for d in range(I)]
    z_peer = [lax.rem(zi + d, O) for d in range(O)]
    z_from = [lax.rem(zi + O - d, O) for d in range(O)]

    def x_id(d):
        return {"fsdp": x_peer[d]}

    def y_id(d):
        return {"dp": zi * I + y_peer[d]}

    def z_id(d):
        return {"dp": z_peer[d] * I + yi}

    core_id = {"section": 1 - core}

    def dp_id(p):
        return {"dp": p}

    def group_id(p):
        return {"fsdp": p // S, "section": p % S}

    others = [dp_id(lax.rem(dp + d, O * I)) for d in range(1, O * I)] + [
        group_id(lax.rem(x * S + core + d, F * S)) for d in range(1, F * S)
    ]
    barrier = pltpu.get_barrier_semaphore()
    for other in others:
        pl.semaphore_signal(barrier, inc=1, device_id=other, device_id_type=MESH)

    sent = []

    def send(src, dst, ssem, rsem, to):
        copy = pltpu.make_async_remote_copy(
            src_ref=src, dst_ref=dst, send_sem=ssem, recv_sem=rsem, device_id=to, device_id_type=MESH
        )
        copy.start()
        sent.append(copy)

    def arrive(src, dst, ssem, rsem, to):
        pltpu.make_async_remote_copy(
            src_ref=src, dst_ref=dst, send_sem=ssem, recv_sem=rsem, device_id=to, device_id_type=MESH
        ).wait_recv()

    def proj_exchange(n, value):
        proj_send[n] = value.astype(BF16)
        for d in range(1, F):
            send(proj_send.at[n], proj_recv.at[n, d], x_send_sem.at[n, d], x_recv_sem.at[n, d], x_id(d))

    def proj_sum(n, value):
        for d in range(1, F):
            arrive(proj_send.at[n], proj_recv.at[n, d], x_send_sem.at[n, d], x_recv_sem.at[n, d], x_id(d))
            value = value + proj_recv[n, d].astype(F32)
        return value

    loads["og"].wait()
    loads["up"].wait()
    loads["prompts"].start()
    loads["frozen"].start()
    slot = T // lengths.shape[0]
    position = lax.broadcasted_iota(jnp.int32, (slot, C), 0)
    for i in range(lengths.shape[0]):
        weight = jnp.where(position < lengths[i], buckets[i].astype(F32) - 1.5, 0.0)
        block = og[i * slot:(i + 1) * slot, :].astype(F32)
        gk[x, i * slot:(i + 1) * slot, :] = (weight * block).astype(BF16)
    mine = gk[x]
    up_part = lax.dot_general(mine, up[...].astype(BF16), NT, preferred_element_type=F32)
    pl.semaphore_wait(barrier, len(others))
    proj_exchange(0, up_part)

    loads["acts"].wait()
    loads["down"].wait()
    a_half[...] = down[...].astype(BF16)
    down_part = jnp.dot(acts[...], a_half[...], preferred_element_type=F32)
    proj_exchange(1, down_part)

    loads["prompts"].wait()
    pd[...] = jnp.dot(prompts[...], a_half[...], preferred_element_type=F32)
    tile_c = min(256, C)

    def frozen_part(owner, put, first=0, last=C // tile_c):
        @pl.loop(first, last)
        def _(t):
            cols = pl.ds(pl.multiple_of(t * tile_c, tile_c), tile_c)
            src = pl.ds(pl.multiple_of(owner * C + t * tile_c, tile_c), tile_c)
            put(cols, jnp.dot(prompts[...], frozen[:, src], preferred_element_type=F32))

    up_half = proj_sum(0, up_part)
    for d in range(1, F):
        send(gk.at[x], gk.at[x], x_send_sem.at[4, d], x_recv_sem.at[4, d], x_id(d))
    up_half_t = up_half.T.astype(BF16)
    up_half = up_half.astype(BF16)
    down_half_t = None

    def core_copy(k):
        return (gbuf.at[k, 1 - core], core_recv.at[k], d_send_sem.at[k, 0], d_recv_sem.at[k, 0], core_id)

    for k in range(K):
        for s in range(S):
            for i in range(I):
                n = (k * S + s) * I + i
                if n < plan.down_units:
                    part = jnp.dot(up_half_t, acts[:, n * U:(n + 1) * U], preferred_element_type=F32)
                elif n < plan.units:
                    if down_half_t is None:
                        down_half_t = proj_sum(1, down_part).T.astype(BF16)
                    m = n - plan.down_units
                    part = jnp.dot(down_half_t, gk[x, :, m * U:(m + 1) * U], preferred_element_type=F32)
                else:
                    part = jnp.zeros((plan.rank, U), F32)
                gbuf[k, s, i] = ADAPTER_SCALE * part
        send(*core_copy(k))
    def y_copy(k, d):
        return (y_send.at[k, d], y_recv.at[k, d], d_send_sem.at[k, d], d_recv_sem.at[k, d], y_id(d))

    def z_copy(k, d):
        e = I + d
        return (z_send.at[k, z_peer[d]], z_recv.at[k, d], d_send_sem.at[k, e], d_recv_sem.at[k, e], z_id(d))

    for k in range(K):
        arrive(*core_copy(k))
        for d in range(I):
            value = gbuf[k, core, y_peer[d]] + core_recv[k, y_peer[d]]
            if d == 0:
                quarter[k] = value
            else:
                y_send[k, d] = value.astype(BF16)
                send(*y_copy(k, d))

    def put_own(cols, value):
        kp_own[:, cols] = value

    loads["frozen"].wait()
    part_rows = plan.rank // O
    tiles_c = C // tile_c

    def share(n, step):
        return step * n // K, (step + 1) * n // K

    for k in range(K):
        first, last = share(tiles_c, K - 1 - k)
        for d in range(1, F):
            def put_other(cols, value, d=d):
                kp_send[d, :, cols] = value.astype(BF16)

            if first < last:
                frozen_part(x_peer[d], put_other, first, last)
        value = quarter[k]
        for d in range(1, I):
            arrive(*y_copy(k, d))
            value = value + y_recv[k, d].astype(F32)
        quarter[k] = value
        for o in range(O):
            z_send[k, o] = value[o * part_rows:(o + 1) * part_rows].astype(BF16)
        for d in range(1, O):
            send(*z_copy(k, d))

    def kp_copy(half, d):
        span = pl.ds(half * (T // 2), T // 2)
        n = (3, 5)[half]
        return (
            kp_send.at[d, span, :], kp_recv.at[d, span, :], x_send_sem.at[n, d], x_recv_sem.at[n, d], x_id(d)
        )

    for d in range(1, F):
        send(*kp_copy(0, d))

    base = I + O

    def ag_z(k, d, slot):
        e = base + d
        return (ag.at[k, core, yi, zi], ag.at[k, core, yi, slot], d_send_sem.at[k, e], d_recv_sem.at[k, e], z_id(d))

    def ag_y(k, d, slot):
        e = base + O + d
        return (ag.at[k, core, yi], ag.at[k, core, slot], d_send_sem.at[k, e], d_recv_sem.at[k, e], y_id(d))

    def ag_core(k, slot):
        e = base + O + I
        return (ag.at[k, core], ag.at[k, slot], d_send_sem.at[k, e], d_recv_sem.at[k, e], core_id)

    squares = jnp.zeros((part_rows, U), F32)
    for k in range(K):
        first, last = share(tiles_c, K - 1 - k)
        if first < last:
            frozen_part(x, put_own, first, last)
        value = quarter[k, pl.ds(pl.multiple_of(zi * part_rows, part_rows), part_rows), :]
        for d in range(1, O):
            arrive(*z_copy(k, d))
            value = value + z_recv[k, d].astype(F32)
        rounded = value.astype(BF16)
        ag[k, core, yi, zi] = rounded
        for d in range(1, O):
            send(*ag_z(k, d, zi))
        value = rounded.astype(F32)
        squares = squares + value * value

    D, G = O * I, F * S
    dp_peer = [lax.rem(dp + d, D) for d in range(D)]
    group = x * S + core
    group_peer = [lax.rem(group + d, G) for d in range(G)]

    def sq_copy(stage, own, slot, d, to):
        return (sq.at[stage, own], sq.at[stage, slot], q_send_sem.at[stage, d], q_recv_sem.at[stage, d], to)

    def sq_send(stage, value, own, peers, to):
        sq[stage, own] = value
        for d in range(1, len(peers)):
            send(*sq_copy(stage, own, own, d, to(peers[d])))

    def sq_sum(stage, own, peers, to):
        count = len(peers)
        for d in range(1, count):
            arrive(*sq_copy(stage, own, lax.rem(own + count - d, count), d, to(peers[d])))
        total = sq[stage, 0]
        for n in range(1, count):
            total = total + sq[stage, n]
        return total

    total = jnp.broadcast_to(jnp.sum(squares, keepdims=True), (8, 128))
    sq_send(0, total, dp, dp_peer, dp_id)

    for k in range(K):
        for d in range(1, O):
            arrive(*ag_z(k, d, z_from[d]))
        for d in range(1, I):
            send(*ag_y(k, d, yi))
    sq_send(1, sq_sum(0, dp, dp_peer, dp_id), group, group_peer, group_id)

    for k in range(K):
        for d in range(1, I):
            arrive(*ag_y(k, d, y_from[d]))
        send(*ag_core(k, core))

    for d in range(1, F):
        arrive(gk.at[x], gk.at[x_from[d]], x_send_sem.at[4, d], x_recv_sem.at[4, d], x_id(d))
    for d in range(1, F):
        send(*kp_copy(1, d))
    tile = plan.tile

    def ig_tile(t):
        span = pl.ds(pl.multiple_of(t * tile, tile), tile)
        value = ADAPTER_SCALE * lax.dot_general(up_half, a_half[span, :], NT, preferred_element_type=F32)
        for p in range(F):
            value = value + lax.dot_general(
                gk[p], frozen[span, p * C:(p + 1) * C], NT, preferred_element_type=F32
            )
        ig[:, span] = value.astype(BF16)

    tiles = W // tile

    def unit_of(n):
        k, s, i = n // (S * I), (n // I) % S, n % I
        return ag[k, s, i].reshape(plan.rank, U)

    low = jnp.zeros((T, plan.rank), F32)
    for k in range(K):
        first, last = share(tiles, k)
        if first < last:
            pl.loop(first, last)(ig_tile)
        arrive(*ag_core(k, 1 - core))
        for n in range(k * S * I, (k + 1) * S * I):
            if n < plan.down_units:
                low = low + lax.dot_general(
                    prompts[:, n * U:(n + 1) * U], unit_of(n), NT, preferred_element_type=F32
                )
    total = sq_sum(1, group, group_peer, group_id)
    norm = jnp.sqrt(total + 1e-12)
    factor = (STEP_RATE * jnp.minimum(1.0, CLIP_NORM / norm))[0:1, 0:1]

    pg[...] = pd[...] - factor * low
    proj_exchange(2, pg[...])

    for n in range(plan.units):
        if n < plan.down_units:
            span = slice(n * U, (n + 1) * U)
            nd[span, :] = down[span, :] - factor * unit_of(n).astype(F32).T
        else:
            span = slice((n - plan.down_units) * U, (n - plan.down_units + 1) * U)
            nu[:, span] = up[:, span] - factor * unit_of(n).astype(F32)

    for d in range(1, F):
        for half in range(2):
            arrive(*kp_copy(half, d))
        kp_own[...] = kp_own[...] + kp_recv[d].astype(F32)
    low_half = (ADAPTER_SCALE * proj_sum(2, pg[...])).astype(BF16)
    keys[...] = (
        kp_own[...] + jnp.dot(low_half, nu[...].astype(BF16), preferred_element_type=F32)
    ).astype(BF16)

    for copy in sent:
        copy.wait_send()


def move_kernel(pieces, *refs):
    sem = refs[-1]
    copies = []
    for n, (which, row, count) in enumerate(pieces):
        src, dst = refs[which], refs[4 + which]
        span = pl.ds(row, count)
        copies.append(pltpu.make_async_copy(src.at[span, :], dst.at[span, :], sem.at[n]))
        copies[-1].start()
    for copy in copies:
        copy.wait()


def per_device(mesh, acts, output_gradient, lengths, buckets, frozen, down, up, prompts):
    T, W = acts.shape
    C = output_gradient.shape[1]
    R = down.shape[1]
    plan = Plan(mesh, T, W, C, R)
    F, S, I, O, K, U = plan.fsdp, plan.cores, plan.inner, plan.outer, plan.chunks, plan.unit
    N = C * F
    smem = pl.BlockSpec(memory_space=pltpu.SMEM)
    hbm = pl.BlockSpec(memory_space=pl.ANY)
    vmem = pl.BlockSpec(memory_space=pltpu.VMEM)
    dma = pltpu.SemaphoreType.DMA
    hops = I + O + O + I + 1
    scratch = [
        pltpu.VMEM((T, W), BF16), pltpu.VMEM((T, C), BF16), pltpu.VMEM((W, N), BF16),
        pltpu.VMEM((W, R), F32), pltpu.VMEM((R, C), F32), pltpu.VMEM((T, W), BF16),
        pltpu.VMEM((W, R), BF16), pltpu.VMEM((F, T, C), BF16),
        pltpu.VMEM((3, T, R), BF16), pltpu.VMEM((3, F, T, R), BF16),
        pltpu.VMEM((T, R), F32), pltpu.VMEM((T, R), F32),
        pltpu.VMEM((T, C), F32), pltpu.VMEM((F, T, C), BF16), pltpu.VMEM((F, T, C), BF16),
        pltpu.VMEM((K, S, I, R, U), F32), pltpu.VMEM((K, I, R, U), F32),
        pltpu.VMEM((K, I, R, U), BF16), pltpu.VMEM((K, I, R, U), BF16),
        pltpu.VMEM((K, R, U), F32),
        pltpu.VMEM((K, O, R // O, U), BF16), pltpu.VMEM((K, O, R // O, U), BF16),
        pltpu.VMEM((K, S, I, O, R // O, U), BF16),
        pltpu.VMEM((2, max(O * I, F * S), 8, 128), F32),
        dma((6,)), dma((6, F)), dma((6, F)), dma((K, hops)), dma((K, hops)),
        dma((2, max(O * I, F * S))), dma((2, max(O * I, F * S))),
    ]
    results = pl.pallas_call(
        functools.partial(kernel, plan),
        out_shape=(
            pltpu.VMEM((T, W), BF16), pltpu.VMEM((W, R), F32), pltpu.VMEM((R, C), F32), pltpu.VMEM((T, C), BF16),
        ),
        in_specs=[smem, smem] + [hbm] * 6,
        out_specs=(vmem,) * 4,
        scratch_shapes=scratch,
        compiler_params=pltpu.CompilerParams(
            collective_id=0, has_side_effects=True, vmem_limit_bytes=48 * 1024 * 1024
        ),
        cost_estimate=pl.CostEstimate(
            flops=2 * T * W * (2 * N + 4 * R), bytes_accessed=2 * (3 * T * W + W * N), transcendentals=0
        ),
        name="adapter_step",
    )(*(
        pltpu.with_memory_space_constraint(a, pltpu.HBM)
        for a in (lengths, buckets, acts, output_gradient, frozen, down, up, prompts)
    ))
    pieces = [(0, n * T // 4, T // 4) for n in range(4)] + [
        (1, n * W // 2, W // 2) for n in range(2)
    ] + [(2, 0, R), (3, 0, T)]
    return pl.pallas_call(
        functools.partial(move_kernel, pieces),
        out_shape=[pltpu.HBM(r.shape, r.dtype) for r in results],
        in_specs=[vmem] * 4,
        out_specs=[hbm] * 4,
        scratch_shapes=[dma((len(pieces),))],
        compiler_params=pltpu.CompilerParams(vmem_limit_bytes=16 * 1024 * 1024),
        name="move_results",
    )(*(pltpu.with_memory_space_constraint(r, pltpu.VMEM) for r in results))


def solution(mesh):
    tokens = P(("dp", "section"), "fsdp")
    return jax.shard_map(
        functools.partial(per_device, mesh),
        mesh=mesh,
        in_specs=(
            tokens, tokens, P(("dp", "section")), P(("dp", "section")),
            P("fsdp", None), P("fsdp", None), P(None, "fsdp"), tokens,
        ),
        out_specs=(tokens, P("fsdp", None), P(None, "fsdp"), tokens),
        check_vma=False,
    )
```
